256 devices in a mesh: kv: 32 (over z, y), seq: 8 (over x, core).
Axes of the slice: x: 4, y: 4, z: 8, core: 2. Of those that a mesh axis runs over, the one named last changes fastest.
Arguments:
- kv_cache: bfloat16 [32, 73728, 576], P('seq', 'kv'), may hold values from -4 to 4
- lengths: int32 [32], P('seq'), may hold values from 4608 to 73728, as said below
- q_nope: bfloat16 [32, 128, 128], P('seq', 'kv'), may hold values from -6 to 6
- q_rope: bfloat16 [32, 128, 64], P('seq', 'kv'), may hold values from -32 to 32
- w_uk: bfloat16 [128, 128, 512], P('kv'), may hold values from -0.75 to 0.75
- w_uv: bfloat16 [128, 512, 128], P('kv'), may hold values from -3 to 3
- w_o: bfloat16 [16384, 7168], P('kv', 'seq'), may hold values from -0.046875 to 0.046875
Outputs:
- layer_out: bfloat16 [32, 7168], P('kv', 'seq')
The draws below stay inside these ranges and needn't reach their ends.
Inputs may be any that keep to these rules, and one draw needn't show every extreme that they name: `lengths`: at least one sequence has all 73728 slots live.
All inputs are finite; a program needn't handle non-finite values.
Results may differ from the reference program's by a relative error of at most 0.025.
Values may be sent and summed in bfloat16 or wider, within the bound.
A program may use at most 64 MiB of HBM per device.

```python
import math
import jax
import jax.numpy as jnp
from jax import lax

H = 128
QK_NOPE = 128
ROPE = 64
KV_RANK = 512
V_HEAD = 128
D_MODEL = 7168
CTX_DEV = 2304
LATENT = 576
SEQS = 32
CTX = 73728
N_KV = 32


def length_draw(key):
    shortest = max(CTX // 16, 1)
    drawn = jax.random.randint(jax.random.fold_in(key, 101), (SEQS,), shortest, CTX + 1)
    chosen = jax.random.randint(jax.random.fold_in(key, 102), (), 0, SEQS)
    return drawn.at[chosen].set(CTX).astype(jnp.int32)


def draw_lengths(key, part):
    return length_draw(key)


def draw_kv_cache(key, part):
    key = jax.random.fold_in(key, 3)
    drawn = jnp.clip(jax.random.normal(key, (SEQS, CTX, LATENT), jnp.float32), -4.0, 4.0)
    return drawn.astype(jnp.bfloat16)


def draw_q_rope(key, part):
    key = jax.random.fold_in(key, 5)
    drawn = jnp.clip(jax.random.normal(key, (SEQS, H, ROPE), jnp.float32), -4.0, 4.0)
    return drawn.astype(jnp.bfloat16)


def levels(key, dims, pieces, least, high):
    def one(position, shards_of):
        steps = jax.random.uniform(jax.random.fold_in(jax.random.fold_in(key, 6), position), (shards_of,), jnp.float32, least / len(pieces), high / len(pieces))
        return jnp.repeat(jnp.exp(steps), dims[position] // shards_of).reshape((-1,) + (1,) * (len(dims) - position - 1))

    level = one(*pieces[0])
    for cut in pieces[1:]:
        level = level * one(*cut)
    return level


def gaussian(own_key, extent, deviation, reach, split=(), held_as=jnp.bfloat16):
    level = levels(own_key, extent, split, -0.22, 0.18) if split else 1.0
    result = jax.random.normal(own_key, extent, jnp.float32) * deviation * level
    return jnp.minimum(jnp.maximum(result, -reach), reach).astype(held_as)


def setup_inputs(seed: int = 0) -> dict:
    streams_of = jax.random.split(jax.random.key(seed), 8)
    return {
        "kv_cache": draw_kv_cache(jax.random.fold_in(streams_of[7], 71), 0),
        "lengths": draw_lengths(jax.random.fold_in(streams_of[7], 71), 0),
        "q_nope": gaussian(streams_of[2], (SEQS, H, QK_NOPE), 1.0, 6.0, ((0, 8), (1, 32))),
        "q_rope": draw_q_rope(jax.random.fold_in(streams_of[7], 71), 0),
        "w_uk": gaussian(streams_of[4], (H, QK_NOPE, KV_RANK), (QK_NOPE // 2) ** -0.5, 0.75, ((0, 32),)),
        "w_uv": gaussian(streams_of[5], (H, KV_RANK, V_HEAD), (max(KV_RANK // 128, 1)) ** -0.5, 3.0, ((0, 32),)),
        "w_o": gaussian(streams_of[6], (H * V_HEAD, D_MODEL), (H * V_HEAD) ** -0.5, 0.046875, ((0, 32), (1, 8))),
    }


def attend_one(packed):
    latent_cache, query_rows, length = packed
    blocks = latent_cache.reshape(N_KV, CTX_DEV, LATENT)
    positions = jnp.arange(CTX, dtype=jnp.int32).reshape(N_KV, CTX_DEV)
    live_mask = (positions < length)[:, None, :]
    score_scale = 1.0 / math.sqrt(QK_NOPE + ROPE)
    scores = jnp.einsum('hl,ktl->kht', query_rows.astype(jnp.float32), blocks.astype(jnp.float32)) * score_scale
    scores = jnp.where(live_mask, scores, -1e+30)
    maxima = lax.optimization_barrier(jnp.max(scores, axis=-1))
    weights = jnp.where(live_mask, jnp.exp(scores - maxima[..., None]), 0.0)
    totals = lax.optimization_barrier(jnp.sum(weights, axis=-1))
    rounded = lax.optimization_barrier(weights.astype(jnp.bfloat16)).astype(jnp.float32)
    partial_out = jnp.einsum('kht,ktl->khl', rounded, blocks.astype(jnp.float32))[..., :KV_RANK]
    normalized = partial_out / jnp.maximum(totals, 1.0)[..., None]
    normalized = lax.optimization_barrier(normalized.astype(jnp.bfloat16)).astype(jnp.float32)
    largest = lax.optimization_barrier(jnp.max(maxima, axis=0))
    factors = jnp.exp(maxima - largest) * totals
    summed = lax.optimization_barrier(jnp.sum(factors, axis=0))
    merged = lax.optimization_barrier(jnp.sum(factors[..., None] * normalized, axis=0)) / summed[:, None]
    return merged.astype(jnp.bfloat16)

def reference(kv_cache, lengths, q_nope, q_rope, w_uk, w_uv, w_o):
    absorbed = jnp.einsum('bhn,hnr->bhr', q_nope.astype(jnp.float32), w_uk.astype(jnp.float32)).astype(jnp.bfloat16)
    absorbed = lax.optimization_barrier(absorbed)
    queries = jnp.concatenate([absorbed, q_rope], axis=-1)
    latents = lax.map(attend_one, (kv_cache, queries, lengths))
    latents = lax.optimization_barrier(latents)
    heads_out = jnp.einsum('bhr,hrv->bhv', latents.astype(jnp.float32), w_uv.astype(jnp.float32)).astype(jnp.bfloat16)
    heads_out = heads_out.reshape(SEQS, H * V_HEAD)
    return jnp.dot(heads_out, w_o, preferred_element_type=jnp.float32).astype(jnp.bfloat16)
```

```python
import functools
import math

import jax
import jax.numpy as jnp
from jax import lax
from jax.experimental import pallas as pl
from jax.experimental.pallas import tpu as pltpu
from jax.sharding import PartitionSpec as P

F32 = jnp.float32
BF16 = jnp.bfloat16
NZ, NY, NS = 8, 4, 8
B, HL = 4, 4
LAST = B - 1
SEQS = NS * B
RANK, ROPE, NOPE, VH = 512, 64, 128, 128
ROWS = B * HL
GROUP = NZ * HL
HEADS = NY * GROUP
LANES = 128
PARTS = RANK // LANES
DEAD, FLOOR = -1e30, -1e29
FAR_FIRST = sorted(range(1, NZ), key=lambda d: (-min(d, NZ - d), d))


def halves(a, c):
    first = lax.broadcasted_iota(jnp.int32, a.shape, 0) < 4
    return (
        jnp.where(first, a, pltpu.roll(c, 4, 0)),
        jnp.where(first, pltpu.roll(a, 4, 0), c),
    )


def take(block, lane):
    return jnp.broadcast_to(block[:, lane:lane + 1], block.shape)


def kernel(
    lengths_hbm, qn_hbm, qr_hbm, kv_hbm, wuk_hbm, wuv_hbm, wo_hbm, out,
    lengths, qn, qr, kvt, vt, wuk, wuv, wo,
    own, g1, g1r, ya, za, spread, around, qall, qrope, qrope3, d1s, d1, tall, t1s, t1, factor, flat, d2s, d2, t2s, t2, deep,
    lat, fall, ff, wide, h2s, h2,
    local, local_kv, sent, r_g1, r_g2, r_a, r_d1, r_t1, r_d2, r_t2, r_f, r_h2,
):
    kv, s = lax.axis_index("kv"), lax.axis_index("seq")
    z, y = kv // NY, kv % NY
    ctx = kvt.shape[2]
    scale = 1.0 / math.sqrt(NOPE + ROPE)

    def at_z(i):
        return {"kv": i * NY + y, "seq": s}

    def at_y(i):
        return {"kv": z * NY + i, "seq": s}

    def at_s(i):
        return {"kv": kv, "seq": i}

    def zs(d):
        return lax.rem(z + d, NZ)

    def ys(d):
        return lax.rem(y + d, NY)

    def ss(d):
        return lax.rem(s + d, NS)

    barrier = pltpu.get_barrier_semaphore()
    peers = (
        [at_z(zs(d)) for d in FAR_FIRST]
        + [at_s(ss(d)) for d in range(1, NS)]
        + [at_y(ys(d)) for d in range(1, NY)]
    )
    for peer in peers:
        pl.semaphore_signal(barrier, inc=1, device_id=peer, device_id_type=pl.DeviceIdType.MESH)

    small = [
        pltpu.make_async_copy(qn_hbm, qn, local.at[0]),
        pltpu.make_async_copy(qr_hbm, qr, local.at[1]),
        pltpu.make_async_copy(wuk_hbm, wuk, local.at[2]),
    ]
    late = [
        pltpu.make_async_copy(wuv_hbm, wuv, local.at[3]),
        pltpu.make_async_copy(wo_hbm, wo, local.at[4]),
        pltpu.make_async_copy(lengths_hbm, lengths, local.at[5]),
    ]
    caches = [
        pltpu.make_async_copy(kv_hbm.at[b], kvt.at[b], local_kv.at[b]) for b in range(B)
    ]
    for copy in small:
        copy.start()

    def send(src, dst, send_sem, recv_sem, to):
        pltpu.make_async_remote_copy(
            src_ref=src, dst_ref=dst, send_sem=send_sem, recv_sem=recv_sem,
            device_id=to, device_id_type=pl.DeviceIdType.MESH,
        ).start()

    def bytes_of(ref, sem):
        return pltpu.make_async_remote_copy(
            src_ref=ref, dst_ref=ref, send_sem=sem, recv_sem=sem,
            device_id=at_z(z), device_id_type=pl.DeviceIdType.MESH,
        )

    def arrive(ref, sem):
        bytes_of(ref, sem).wait_recv()

    def yrows(i):
        return pl.ds(pl.multiple_of(i * GROUP, GROUP), GROUP)

    for copy in small:
        copy.wait()
    for copy in caches + late:
        copy.start()
    head = lax.broadcasted_iota(jnp.int32, (ROWS, 1), 0) % HL
    q16 = qn[...].astype(F32).reshape(ROWS, NOPE).astype(BF16)
    absorbed = jnp.zeros((ROWS, RANK), F32)
    for h in range(HL):
        product = jnp.dot(q16, wuk[h], preferred_element_type=F32)
        absorbed = jnp.where(head == h, product, absorbed)
    rope = qr[...].astype(F32).reshape(ROWS, ROPE)
    for j in range(PARTS):
        own[pl.ds(j, ROWS, stride=PARTS)] = absorbed[:, j * LANES:(j + 1) * LANES]
    g1[z] = own[...].astype(BF16).reshape(B, HL * PARTS, LANES)
    ya[y, 0] = g1[z, LAST]
    g1r[z] = jnp.concatenate([rope, jnp.zeros((ROWS, LANES - ROPE), F32)], axis=1).astype(BF16)
    ya[y, 1] = g1r[z]

    pl.semaphore_wait(barrier, len(peers))

    for d in FAR_FIRST:
        send(g1.at[z, 0], g1.at[z, 0], sent.at[1], r_g1.at[1], at_z(zs(d)))
    for d in (2, 1, 3):
        send(ya.at[y], ya.at[y], sent.at[10], r_a.at[0], at_y(ys(d)))
    for d in FAR_FIRST:
        send(g1r.at[z], g1r.at[z], sent.at[0], r_g1.at[0], at_z(zs(d)))
    for d in FAR_FIRST:
        rest = g1.at[z, pl.ds(1, LAST - 1)]
        send(rest, rest, sent.at[1], r_g1.at[2], at_z(zs(d)))

    def turn_cache(b):
        caches[b].wait()
        vt[b] = kvt[b, :RANK].T

    def pass_on(b):
        spread[b] = g1[:, b].astype(F32).reshape(GROUP * PARTS, LANES)
        parts = [spread[b, pl.ds(j, GROUP, stride=PARTS)] for j in range(PARTS)]
        part = qall.at[b, yrows(y)]
        part[...] = jnp.concatenate(parts, axis=1).astype(BF16)
        for d in (2, 1, 3):
            send(part, part, sent.at[2], r_g2.at[b], at_y(ys(d)))

    turn_cache(0)
    arrive(ya.at[pl.ds(1, NY - 1)], r_a.at[0])
    around[...] = ya[:, 0].astype(F32).reshape(NY * ROWS, LANES)
    parts = [around[pl.ds(j, ROWS, stride=PARTS)] for j in range(PARTS)]
    tails = [ya[i, 1].astype(F32)[8:] for i in range(NY)]
    tail = jnp.concatenate(
        [halves(tails[0], tails[1])[1], halves(tails[2], tails[3])[1]], axis=0
    )
    za[z] = jnp.concatenate(parts + [tail], axis=1).astype(BF16)
    for d in FAR_FIRST:
        send(za.at[z], za.at[z], sent.at[11], r_a.at[1], at_z(zs(d)))
    turn_cache(1)
    arrive(g1.at[pl.ds(1, NZ - 1), 0], r_g1.at[1])
    pass_on(0)
    arrive(g1r.at[pl.ds(1, NZ - 1)], r_g1.at[0])
    for k in range(0, NZ, 4):
        blocks = [g1r[k + j].astype(F32) for j in range(4)]
        for p in range(B // 2):
            rows = slice(8 * p, 8 * p + 8)
            low = halves(blocks[0][rows], blocks[1][rows])
            high = halves(blocks[2][rows], blocks[3][rows])
            pair = [jnp.concatenate([low[i], high[i]], axis=0) for i in range(2)]
            where = pl.ds(pl.multiple_of(y * GROUP + k * HL, 16), 16)
            both = pair[0] + pltpu.roll(pair[1], ROPE, 1)
            qrope[where, p * LANES:(p + 1) * LANES] = both.astype(BF16)
    part = qrope.at[yrows(y)]
    for d in (2, 1, 3):
        send(part, part, sent.at[3], r_g2.at[LAST], at_y(ys(d)))
    arrive(g1.at[pl.ds(1, NZ - 1), pl.ds(1, LAST - 1)], r_g1.at[2])
    for b in range(1, LAST):
        pass_on(b)

    for b in range(2, B):
        turn_cache(b)

    def turn():
        arrive(za.at[pl.ds(1, NZ - 1)], r_a.at[1])
        for k in range(0, NZ, 4):
            blocks = [za[k + j].astype(F32) for j in range(4)]
            for p in range(NY // 2):
                rows = slice(8 * p, 8 * p + 8)
                low = halves(blocks[0][rows], blocks[1][rows])
                high = halves(blocks[2][rows], blocks[3][rows])
                for i in range(2):
                    both = jnp.concatenate([low[i], high[i]], axis=0).astype(BF16)
                    first = (2 * p + i) * GROUP + k * HL
                    qall[LAST, first:first + 16] = both[:, :RANK]
                    qrope3[first:first + 16] = both[:, RANK:]

    even = lax.broadcasted_iota(jnp.int32, (NZ, LANES), 1) % 2 == 0

    def pack(b, maxima, totals):
        lane = lax.broadcasted_iota(jnp.int32, (HEADS, LANES), 1)
        tall[b] = jnp.where(lane == 0, maxima, jnp.where(lane == 1, totals, 0.0))
        for i in range(NY):
            block = tall[b, pl.ds(i * GROUP, NZ, stride=HL)]
            for h in range(1, HL):
                block = block + pltpu.roll(tall[b, pl.ds(i * GROUP + h, NZ, stride=HL)], 2 * h, 1)
            t1s[b, i] = block

    def join(b):
        t1[b, y] = t1s[b, y]
        d1[b, y] = d1s[b, yrows(y)]
        arrive(t1.at[b, pl.ds(1, NY - 1)], r_t1.at[b])
        stats = [t1[b, i] for i in range(NY)]
        largest = functools.reduce(jnp.maximum, stats)
        factors = [jnp.exp(t - largest) * pltpu.roll(t, LANES - 1, 1) for t in stats]
        summed = sum(factors)
        inverse = 1.0 / jnp.maximum(summed, 1.0)
        joined = jnp.where(even, largest, pltpu.roll(summed, 1, 1))
        for i in range(NZ):
            t2s[b, i] = joined[i:i + 1]
        for d in FAR_FIRST:
            i = zs(d)
            send(t2s.at[b, i], t2.at[b, z], sent.at[7], r_t2.at[b], at_z(i))
        for i in range(NY):
            share = factors[i] * inverse
            for h in range(HL):
                factor[b, i, pl.ds(h, NZ, stride=HL)] = take(share, 2 * h)
        arrive(d1.at[b, pl.ds(1, NY - 1)], r_d1.at[b])
        total = 0.0
        for i in range(NY):
            share = jnp.concatenate([factor[b, i]] * PARTS, axis=1)
            total = total + share * d1[b, i].astype(F32)
        for j in range(PARTS):
            flat[b, pl.ds(j, GROUP, stride=PARTS)] = total[:, j * LANES:(j + 1) * LANES]
        d2s[b] = flat[b].astype(BF16).reshape(NZ, ROWS, LANES)
        for d in FAR_FIRST:
            i = zs(d)
            send(d2s.at[b, i], d2.at[b, z], sent.at[6], r_d2.at[b], at_z(i))

    def finish(b):
        t2[b, z] = t2s[b, z]
        d2[b, z] = d2s[b, z]
        arrive(t2.at[b, pl.ds(1, NZ - 1)], r_t2.at[b])
        stats = jnp.concatenate([t2[b, i] for i in range(NZ)], axis=0)
        largest = jnp.max(stats, axis=0, keepdims=True)
        factors = jnp.exp(stats - largest) * pltpu.roll(stats, LANES - 1, 1)
        summed = jnp.sum(factors, axis=0, keepdims=True)
        shares = factors / jnp.maximum(summed, 1.0)
        arrive(d2.at[b, pl.ds(1, NZ - 1)], r_d2.at[b])
        deep[b] = d2[b].astype(F32).reshape(NZ * ROWS, LANES)
        for h in range(HL):
            share = take(shares, 2 * h)
            for j in range(PARTS):
                rows = deep[b, pl.ds(h * PARTS + j, NZ, stride=ROWS)]
                row = jnp.sum(share * rows, axis=0, keepdims=True)
                lat[b * HL + h:b * HL + h + 1, j * LANES:(j + 1) * LANES] = row

    first_slot = kv * ctx
    late[2].wait()

    def scores_of(b):
        if b == LAST:
            turn()
            tail = qrope3[:, :ROPE]
        else:
            arrive(qall.at[b, pl.ds(0, HEADS - GROUP)], r_g2.at[b])
            if b == 0:
                arrive(qrope.at[pl.ds(0, HEADS - GROUP)], r_g2.at[LAST])
            tail = qrope[:, b * ROPE:(b + 1) * ROPE]
        scores = jnp.dot(
            qall[b], kvt[b, :RANK], preferred_element_type=F32
        ) + jnp.dot(tail, kvt[b, RANK:], preferred_element_type=F32)
        slot = lax.broadcasted_iota(jnp.int32, (1, ctx), 1)
        return jnp.where(slot < lengths[b] - first_slot, scores, DEAD)

    scores = scores_of(0)
    for b in range(B):
        following = scores_of(b + 1) if b + 1 < B else None
        m = jnp.max(scores, axis=1, keepdims=True)
        weights = jnp.exp2((scores - jnp.maximum(m, FLOOR)) * (scale * math.log2(math.e)))
        l = jnp.sum(weights, axis=1, keepdims=True)
        weights = weights.astype(BF16)
        inverse = 1.0 / jnp.maximum(l, 1.0)
        pack(b, m * scale, l)
        step = RANK // 2 if b == LAST else RANK
        for c in range(0, RANK, step):
            total = jnp.dot(weights, vt[b, :, c:c + step], preferred_element_type=F32)
            d1s[b, :, c:c + step] = (total * inverse).astype(BF16)
            for d in (2, 1, 3):
                i = ys(d)
                if c == 0:
                    send(t1s.at[b, i], t1.at[b, y], sent.at[5], r_t1.at[b], at_y(i))
                cols = pl.ds(c, step)
                send(
                    d1s.at[b, yrows(i), cols], d1.at[b, y, :, cols],
                    sent.at[4], r_d1.at[b], at_y(i),
                )
        scores = following
    for b in range(B):
        join(b)
    for b in range(B):
        finish(b)
    latent = lat[...].astype(BF16)

    late[0].wait()
    heads = jnp.zeros((ROWS, VH), F32)
    for h in range(HL):
        product = jnp.dot(latent, wuv[h], preferred_element_type=F32)
        heads = jnp.where(head == h, product, heads)
    fall[s] = heads.astype(BF16)
    for d in (4, 3, 5, 2, 6, 1, 7):
        send(fall.at[s], fall.at[s], sent.at[8], r_f, at_s(ss(d)))
    arrive(fall.at[pl.ds(1, NS - 1)], r_f)
    ff[...] = fall[...].astype(F32).reshape(NS * ROWS, VH)
    late[1].wait()
    x = jnp.concatenate(
        [
            jnp.concatenate(
                [ff[pl.ds(b * HL + h, NS, stride=ROWS)] for h in range(HL)], axis=1
            )
            for b in range(B)
        ],
        axis=0,
    ).astype(BF16)
    product = jnp.dot(x, wo[...], preferred_element_type=F32)
    pieces = product.shape[1] // LANES
    wide[...] = jnp.zeros(wide.shape, F32)
    for j in range(pieces):
        wide[pl.ds(j, SEQS, stride=8)] = product[:, j * LANES:(j + 1) * LANES]
    h2s[...] = wide[...].reshape(h2s.shape).astype(BF16)
    for dz, dy in sorted(
        ((dz, dy) for dz in range(NZ) for dy in range(NY) if dz or dy),
        key=lambda d: (-min(d[0], NZ - d[0]) - min(d[1], NY - d[1]), d),
    ):
        i, j = zs(dz), ys(dy)
        send(h2s.at[j * NZ + i], h2.at[kv], sent.at[9], r_h2, {"kv": i * NY + j, "seq": s})
    h2[kv] = h2s[y * NZ + z]
    arrive(h2.at[pl.ds(1, NZ * NY - 1)], r_h2)
    total = jnp.sum(h2[...].astype(F32), axis=0)
    out[...] = jnp.concatenate([total[j:j + 1] for j in range(pieces)], axis=1).astype(
        BF16
    )
    all_sent = [
        g1r.at[pl.ds(1, NZ - 1)],
        g1.at[pl.ds(1, NZ - 1), pl.ds(0, LAST)],
        qall.at[pl.ds(0, LAST), pl.ds(0, HEADS - GROUP)],
        qrope.at[pl.ds(0, HEADS - GROUP)],
        d1s.at[:, pl.ds(0, HEADS - GROUP)],
        t1s.at[:, pl.ds(1, NY - 1)],
        d2s.at[:, pl.ds(1, NZ - 1)],
        t2s.at[:, pl.ds(1, NZ - 1)],
        fall.at[pl.ds(1, NS - 1)],
        h2s.at[pl.ds(1, NZ * NY - 1)],
        ya.at[pl.ds(1, NY - 1)],
        za.at[pl.ds(1, NZ - 1)],
    ]
    for i, ref in enumerate(all_sent):
        bytes_of(ref, sent.at[i]).wait_send()


def per_device(kv_cache, lengths, q_nope, q_rope, w_uk, w_uv, w_o):
    ctx = kv_cache.shape[1]
    dmodel = w_o.shape[1]
    dma = pltpu.SemaphoreType.DMA
    anywhere = pl.BlockSpec(memory_space=pl.ANY)
    return pl.pallas_call(
        kernel,
        out_shape=jax.ShapeDtypeStruct((1, dmodel), BF16),
        in_specs=[anywhere] * 7,
        out_specs=pl.BlockSpec(memory_space=pltpu.VMEM),
        scratch_shapes=[
            pltpu.SMEM((B,), jnp.int32),
            pltpu.VMEM((B, HL, NOPE), BF16),
            pltpu.VMEM((B, HL, ROPE), BF16),
            pltpu.VMEM((B, RANK + ROPE, ctx), BF16),
            pltpu.VMEM((B, ctx, RANK), BF16),
            pltpu.VMEM((HL, NOPE, RANK), BF16),
            pltpu.VMEM((HL, RANK, VH), BF16),
            pltpu.VMEM((HL * VH, dmodel), BF16),
            pltpu.VMEM((ROWS * PARTS, LANES), F32),
            pltpu.VMEM((NZ, B, HL * PARTS, LANES), BF16),
            pltpu.VMEM((NZ, ROWS, LANES), BF16),
            pltpu.VMEM((NY, 2, ROWS, LANES), BF16),
            pltpu.VMEM((NZ, ROWS, RANK + LANES), BF16),
            pltpu.VMEM((B, GROUP * PARTS, LANES), F32),
            pltpu.VMEM((NY * ROWS, LANES), F32),
            pltpu.VMEM((B, HEADS, RANK), BF16),
            pltpu.VMEM((HEADS, B * ROPE), BF16),
            pltpu.VMEM((HEADS, LANES), BF16),
            pltpu.VMEM((B, HEADS, RANK), BF16),
            pltpu.VMEM((B, NY, GROUP, RANK), BF16),
            pltpu.VMEM((B, HEADS, LANES), F32),
            pltpu.VMEM((B, NY, NZ, LANES), F32),
            pltpu.VMEM((B, NY, NZ, LANES), F32),
            pltpu.VMEM((B, NY, GROUP, LANES), F32),
            pltpu.VMEM((B, GROUP * PARTS, LANES), F32),
            pltpu.VMEM((B, NZ, ROWS, LANES), BF16),
            pltpu.VMEM((B, NZ, ROWS, LANES), BF16),
            pltpu.VMEM((B, NZ, 1, LANES), F32),
            pltpu.VMEM((B, NZ, 1, LANES), F32),
            pltpu.VMEM((B, NZ * ROWS, LANES), F32),
            pltpu.VMEM((ROWS, RANK), F32),
            pltpu.VMEM((NS, ROWS, VH), BF16),
            pltpu.VMEM((NS * ROWS, VH), F32),
            pltpu.VMEM((SEQS * 8, LANES), F32),
            pltpu.VMEM((SEQS, 8, LANES), BF16),
            pltpu.VMEM((SEQS, 8, LANES), BF16),
            dma((6,)), dma((B,)), dma((12,)),
            dma((3,)), dma((B,)), dma((2,)),
            dma((B,)), dma((B,)), dma((B,)), dma((B,)),
            dma, dma,
        ],
        compiler_params=pltpu.CompilerParams(
            collective_id=0, has_side_effects=True, vmem_limit_bytes=62 * 1024 * 1024
        ),
    )(lengths, q_nope, q_rope, jnp.swapaxes(kv_cache, 1, 2), w_uk, w_uv, w_o)


def solution(mesh):
    return jax.shard_map(
        per_device,
        mesh=mesh,
        in_specs=(
            P("seq", "kv", None),
            P("seq"),
            P("seq", "kv", None),
            P("seq", "kv", None),
            P("kv", None, None),
            P("kv", None, None),
            P("kv", "seq"),
        ),
        out_specs=P("kv", "seq"),
        check_vma=False,
    )
```

```python
import functools
import math

import jax
import jax.numpy as jnp
from jax import lax
from jax.experimental import pallas as pl
from jax.experimental.pallas import tpu as pltpu
from jax.sharding import PartitionSpec as P

F32 = jnp.float32
BF16 = jnp.bfloat16
NZ, NY, NS = 8, 4, 8
B, HL = 4, 4
LAST = B - 1
SEQS = NS * B
RANK, ROPE, NOPE, VH = 512, 64, 128, 128
ROWS = B * HL
GROUP = NZ * HL
HEADS = NY * GROUP
LANES = 128
PARTS = RANK // LANES
DEAD, FLOOR = -1e30, -1e29
FAR_FIRST = sorted(range(1, NZ), key=lambda d: (-min(d, NZ - d), d))


def halves(a, c):
    first = lax.broadcasted_iota(jnp.int32, a.shape, 0) < 4
    return (
        jnp.where(first, a, pltpu.roll(c, 4, 0)),
        jnp.where(first, pltpu.roll(a, 4, 0), c),
    )


def take(block, lane):
    return jnp.broadcast_to(block[:, lane:lane + 1], block.shape)


def kernel(
    lengths_hbm, qn_hbm, qr_hbm, kv_hbm, wuk_hbm, wuv_hbm, wo_hbm, out,
    lengths, qn, qr, kvt, vt, wuk, wuv, wo,
    own, g1, g1r, ya, za, spread, around, qall, qrope, qrope3, e1s, e1, u1s, u1, fz, f2, e2s, e2, u2s, u2, d1s, d1, tall, t1s, t1, factor, flat, d2s, d2, t2s, t2, deep,
    lat, fall, ff, wide, h2s, h2,
    local, local_kv, sent, r_g1, r_g2, r_a, r_e, r_d1, r_t1, r_d2, r_t2, r_f, r_h2,
):
    kv, s = lax.axis_index("kv"), lax.axis_index("seq")
    z, y = kv // NY, kv % NY
    ctx = kvt.shape[2]
    scale = 1.0 / math.sqrt(NOPE + ROPE)

    def at_z(i):
        return {"kv": i * NY + y, "seq": s}

    def at_y(i):
        return {"kv": z * NY + i, "seq": s}

    def at_s(i):
        return {"kv": kv, "seq": i}

    def zs(d):
        return lax.rem(z + d, NZ)

    def ys(d):
        return lax.rem(y + d, NY)

    def ss(d):
        return lax.rem(s + d, NS)

    barrier = pltpu.get_barrier_semaphore()
    peers = (
        [at_z(zs(d)) for d in FAR_FIRST]
        + [at_s(ss(d)) for d in range(1, NS)]
        + [at_y(ys(d)) for d in range(1, NY)]
    )
    for peer in peers:
        pl.semaphore_signal(barrier, inc=1, device_id=peer, device_id_type=pl.DeviceIdType.MESH)

    small = [
        pltpu.make_async_copy(qn_hbm, qn, local.at[0]),
        pltpu.make_async_copy(qr_hbm, qr, local.at[1]),
        pltpu.make_async_copy(wuk_hbm, wuk, local.at[2]),
    ]
    late = [
        pltpu.make_async_copy(wuv_hbm, wuv, local.at[3]),
        pltpu.make_async_copy(wo_hbm, wo, local.at[4]),
        pltpu.make_async_copy(lengths_hbm, lengths, local.at[5]),
    ]
    caches = [
        pltpu.make_async_copy(kv_hbm.at[b], kvt.at[b], local_kv.at[b]) for b in range(B)
    ]
    for copy in small:
        copy.start()

    def send(src, dst, send_sem, recv_sem, to):
        pltpu.make_async_remote_copy(
            src_ref=src, dst_ref=dst, send_sem=send_sem, recv_sem=recv_sem,
            device_id=to, device_id_type=pl.DeviceIdType.MESH,
        ).start()

    def bytes_of(ref, sem):
        return pltpu.make_async_remote_copy(
            src_ref=ref, dst_ref=ref, send_sem=sem, recv_sem=sem,
            device_id=at_z(z), device_id_type=pl.DeviceIdType.MESH,
        )

    def arrive(ref, sem):
        bytes_of(ref, sem).wait_recv()

    def yrows(i):
        return pl.ds(pl.multiple_of(i * GROUP, GROUP), GROUP)

    for copy in small:
        copy.wait()
    for copy in caches + late:
        copy.start()
    head = lax.broadcasted_iota(jnp.int32, (ROWS, 1), 0) % HL
    q16 = qn[...].astype(F32).reshape(ROWS, NOPE).astype(BF16)
    absorbed = jnp.zeros((ROWS, RANK), F32)
    for h in range(HL):
        product = jnp.dot(q16, wuk[h], preferred_element_type=F32)
        absorbed = jnp.where(head == h, product, absorbed)
    rope = qr[...].astype(F32).reshape(ROWS, ROPE)
    for j in range(PARTS):
        own[pl.ds(j, ROWS, stride=PARTS)] = absorbed[:, j * LANES:(j + 1) * LANES]
    g1[z] = own[...].astype(BF16).reshape(B, HL * PARTS, LANES)
    ya[y, 0] = g1[z, LAST]
    g1r[z] = jnp.concatenate([rope, jnp.zeros((ROWS, LANES - ROPE), F32)], axis=1).astype(BF16)
    ya[y, 1] = g1r[z]

    pl.semaphore_wait(barrier, len(peers))

    for d in FAR_FIRST:
        send(g1.at[z, 0], g1.at[z, 0], sent.at[1], r_g1.at[1], at_z(zs(d)))
    for d in (2, 1, 3):
        send(ya.at[y], ya.at[y], sent.at[10], r_a.at[0], at_y(ys(d)))
    for d in FAR_FIRST:
        send(g1r.at[z], g1r.at[z], sent.at[0], r_g1.at[0], at_z(zs(d)))
    for d in FAR_FIRST:
        rest = g1.at[z, pl.ds(1, LAST - 1)]
        send(rest, rest, sent.at[1], r_g1.at[2], at_z(zs(d)))

    def turn_cache(b):
        caches[b].wait()
        vt[b] = kvt[b, :RANK].T

    def pass_on(b):
        spread[b] = g1[:, b].astype(F32).reshape(GROUP * PARTS, LANES)
        parts = [spread[b, pl.ds(j, GROUP, stride=PARTS)] for j in range(PARTS)]
        part = qall.at[b, yrows(y)]
        part[...] = jnp.concatenate(parts, axis=1).astype(BF16)
        for d in (2, 1, 3):
            send(part, part, sent.at[2], r_g2.at[b], at_y(ys(d)))

    turn_cache(0)
    arrive(ya.at[pl.ds(1, NY - 1)], r_a.at[0])
    around[...] = ya[:, 0].astype(F32).reshape(NY * ROWS, LANES)
    parts = [around[pl.ds(j, ROWS, stride=PARTS)] for j in range(PARTS)]
    tails = [ya[i, 1].astype(F32)[8:] for i in range(NY)]
    tail = jnp.concatenate(
        [halves(tails[0], tails[1])[1], halves(tails[2], tails[3])[1]], axis=0
    )
    za[z] = jnp.concatenate(parts + [tail], axis=1).astype(BF16)
    for d in FAR_FIRST:
        send(za.at[z], za.at[z], sent.at[11], r_a.at[1], at_z(zs(d)))
    turn_cache(1)
    arrive(g1.at[pl.ds(1, NZ - 1), 0], r_g1.at[1])
    pass_on(0)
    arrive(g1r.at[pl.ds(1, NZ - 1)], r_g1.at[0])
    for k in range(0, NZ, 4):
        blocks = [g1r[k + j].astype(F32) for j in range(4)]
        for p in range(B // 2):
            rows = slice(8 * p, 8 * p + 8)
            low = halves(blocks[0][rows], blocks[1][rows])
            high = halves(blocks[2][rows], blocks[3][rows])
            pair = [jnp.concatenate([low[i], high[i]], axis=0) for i in range(2)]
            where = pl.ds(pl.multiple_of(y * GROUP + k * HL, 16), 16)
            both = pair[0] + pltpu.roll(pair[1], ROPE, 1)
            qrope[where, p * LANES:(p + 1) * LANES] = both.astype(BF16)
    part = qrope.at[yrows(y)]
    for d in (2, 1, 3):
        send(part, part, sent.at[3], r_g2.at[LAST], at_y(ys(d)))
    arrive(g1.at[pl.ds(1, NZ - 1), pl.ds(1, LAST - 1)], r_g1.at[2])
    for b in range(1, LAST):
        pass_on(b)

    for b in range(2, B):
        turn_cache(b)

    def turn():
        arrive(za.at[pl.ds(1, NZ - 1)], r_a.at[1])
        for k in range(0, NZ, 4):
            blocks = [za[k + j].astype(F32) for j in range(4)]
            for p in range(NY // 2):
                rows = slice(8 * p, 8 * p + 8)
                low = halves(blocks[0][rows], blocks[1][rows])
                high = halves(blocks[2][rows], blocks[3][rows])
                for i in range(2):
                    both = jnp.concatenate([low[i], high[i]], axis=0).astype(BF16)
                    first = (2 * p + i) * GROUP + k * HL
                    qall[LAST, first:first + 16] = both[:, :RANK]
                    qrope3[first:first + 16] = both[:, RANK:]

    even = lax.broadcasted_iota(jnp.int32, (NZ, LANES), 1) % 2 == 0

    def pack(b, maxima, totals):
        lane = lax.broadcasted_iota(jnp.int32, (HEADS, LANES), 1)
        tall[b] = jnp.where(lane == 0, maxima, jnp.where(lane == 1, totals, 0.0))
        for i in range(NY):
            block = tall[b, pl.ds(i * GROUP, NZ, stride=HL)]
            for h in range(1, HL):
                block = block + pltpu.roll(tall[b, pl.ds(i * GROUP + h, NZ, stride=HL)], 2 * h, 1)
            t1s[b, i] = block

    def pack_z(maxima, totals):
        lane = lax.broadcasted_iota(jnp.int32, (HEADS, LANES), 1)
        tall[0] = jnp.where(lane == 0, maxima, jnp.where(lane == 1, totals, 0.0))
        block = tall[0, pl.ds(0, NZ, stride=HL)]
        for r in range(1, ROWS):
            first = (r // HL) * GROUP + r % HL
            block = block + pltpu.roll(tall[0, pl.ds(first, NZ, stride=HL)], 2 * r, 1)
        for i in range(NZ):
            u1s[i] = block[i:i + 1]

    def leave_z(outputs):
        for k in range(NZ // 2):
            blocks = [outputs[i * GROUP + 8 * k:i * GROUP + 8 * k + 8] for i in range(NY)]
            low, high = halves(blocks[0], blocks[1]), halves(blocks[2], blocks[3])
            for i in range(2):
                e1s[2 * k + i] = jnp.concatenate([low[i], high[i]], axis=0).astype(BF16)
        for d in FAR_FIRST:
            i = zs(d)
            send(u1s.at[i], u1.at[z], sent.at[12], r_e.at[0], at_z(i))
            send(e1s.at[i], e1.at[z], sent.at[13], r_e.at[1], at_z(i))

    def join_z():
        u1[z] = u1s[z]
        e1[z] = e1s[z]
        arrive(u1.at[pl.ds(1, NZ - 1)], r_e.at[0])
        stats = jnp.concatenate([u1[i] for i in range(NZ)], axis=0)
        largest = jnp.broadcast_to(jnp.max(stats, axis=0, keepdims=True), stats.shape)
        factors = jnp.exp(stats - largest) * pltpu.roll(stats, LANES - 1, 1)
        summed = jnp.broadcast_to(jnp.sum(factors, axis=0, keepdims=True), stats.shape)
        shares = factors / jnp.maximum(summed, 1.0)
        u2s[...] = jnp.where(even, largest, pltpu.roll(summed, 1, 1))[:1]
        for r in range(ROWS):
            fz[pl.ds(r, NZ, stride=ROWS)] = take(shares, 2 * r)
        arrive(e1.at[pl.ds(1, NZ - 1)], r_e.at[1])
        total = 0.0
        for i in range(NZ):
            share = jnp.concatenate([fz[i * ROWS:(i + 1) * ROWS]] * PARTS, axis=1)
            total = total + share * e1[i].astype(F32)
        for j in range(PARTS):
            f2[pl.ds(j, ROWS, stride=PARTS)] = total[:, j * LANES:(j + 1) * LANES]
        e2s[...] = f2[...].astype(BF16).reshape(NY, ROWS, LANES)
        for d in (2, 1, 3):
            i = ys(d)
            send(u2s, u2.at[y], sent.at[14], r_e.at[2], at_y(i))
            send(e2s.at[i], e2.at[y], sent.at[15], r_e.at[3], at_y(i))

    def finish_z():
        u2[y] = u2s[...]
        e2[y] = e2s[y]
        arrive(u2.at[pl.ds(1, NY - 1)], r_e.at[2])
        rows = [u2[i] for i in range(NY)] + [jnp.full((NZ - NY, LANES), DEAD, F32)]
        stats = jnp.concatenate(rows, axis=0)
        stats = pltpu.roll(stats, lax.rem(LANES - 2 * HL * y, LANES), 1)
        largest = jnp.max(stats, axis=0, keepdims=True)
        factors = jnp.exp(stats - largest) * pltpu.roll(stats, LANES - 1, 1)
        summed = jnp.sum(factors, axis=0, keepdims=True)
        shares = factors / jnp.maximum(summed, 1.0)
        arrive(e2.at[pl.ds(1, NY - 1)], r_e.at[3])
        f2[...] = e2[...].astype(F32).reshape(NY * ROWS, LANES)
        for h in range(HL):
            share = take(shares, 2 * h)[:NY]
            for j in range(PARTS):
                rows = f2[pl.ds(h * PARTS + j, NY, stride=ROWS)]
                row = jnp.sum(share * rows, axis=0, keepdims=True)
                lat[h:h + 1, j * LANES:(j + 1) * LANES] = row

    def join(b):
        t1[b, y] = t1s[b, y]
        d1[b, y] = d1s[b, yrows(y)]
        arrive(t1.at[b, pl.ds(1, NY - 1)], r_t1.at[b])
        stats = [t1[b, i] for i in range(NY)]
        largest = functools.reduce(jnp.maximum, stats)
        factors = [jnp.exp(t - largest) * pltpu.roll(t, LANES - 1, 1) for t in stats]
        summed = sum(factors)
        inverse = 1.0 / jnp.maximum(summed, 1.0)
        joined = jnp.where(even, largest, pltpu.roll(summed, 1, 1))
        for i in range(NZ):
            t2s[b, i] = joined[i:i + 1]
        for d in FAR_FIRST:
            i = zs(d)
            send(t2s.at[b, i], t2.at[b, z], sent.at[7], r_t2.at[b], at_z(i))
        for i in range(NY):
            share = factors[i] * inverse
            for h in range(HL):
                factor[b, i, pl.ds(h, NZ, stride=HL)] = take(share, 2 * h)
        arrive(d1.at[b, pl.ds(1, NY - 1)], r_d1.at[b])
        total = 0.0
        for i in range(NY):
            share = jnp.concatenate([factor[b, i]] * PARTS, axis=1)
            total = total + share * d1[b, i].astype(F32)
        for j in range(PARTS):
            flat[b, pl.ds(j, GROUP, stride=PARTS)] = total[:, j * LANES:(j + 1) * LANES]
        d2s[b] = flat[b].astype(BF16).reshape(NZ, ROWS, LANES)
        for d in FAR_FIRST:
            i = zs(d)
            send(d2s.at[b, i], d2.at[b, z], sent.at[6], r_d2.at[b], at_z(i))

    def finish(b):
        t2[b, z] = t2s[b, z]
        d2[b, z] = d2s[b, z]
        arrive(t2.at[b, pl.ds(1, NZ - 1)], r_t2.at[b])
        stats = jnp.concatenate([t2[b, i] for i in range(NZ)], axis=0)
        largest = jnp.max(stats, axis=0, keepdims=True)
        factors = jnp.exp(stats - largest) * pltpu.roll(stats, LANES - 1, 1)
        summed = jnp.sum(factors, axis=0, keepdims=True)
        shares = factors / jnp.maximum(summed, 1.0)
        arrive(d2.at[b, pl.ds(1, NZ - 1)], r_d2.at[b])
        deep[b] = d2[b].astype(F32).reshape(NZ * ROWS, LANES)
        for h in range(HL):
            share = take(shares, 2 * h)
            for j in range(PARTS):
                rows = deep[b, pl.ds(h * PARTS + j, NZ, stride=ROWS)]
                row = jnp.sum(share * rows, axis=0, keepdims=True)
                lat[b * HL + h:b * HL + h + 1, j * LANES:(j + 1) * LANES] = row

    first_slot = kv * ctx
    late[2].wait()

    def scores_of(b):
        if b == LAST:
            turn()
            tail = qrope3[:, :ROPE]
        else:
            arrive(qall.at[b, pl.ds(0, HEADS - GROUP)], r_g2.at[b])
            if b == 0:
                arrive(qrope.at[pl.ds(0, HEADS - GROUP)], r_g2.at[LAST])
            tail = qrope[:, b * ROPE:(b + 1) * ROPE]
        scores = jnp.dot(
            qall[b], kvt[b, :RANK], preferred_element_type=F32
        ) + jnp.dot(tail, kvt[b, RANK:], preferred_element_type=F32)
        slot = lax.broadcasted_iota(jnp.int32, (1, ctx), 1)
        return jnp.where(slot < lengths[b] - first_slot, scores, DEAD)

    scores = scores_of(0)
    for b in range(B):
        following = scores_of(b + 1) if b + 1 < B else None
        m = jnp.max(scores, axis=1, keepdims=True)
        weights = jnp.exp2((scores - jnp.maximum(m, FLOOR)) * (scale * math.log2(math.e)))
        l = jnp.sum(weights, axis=1, keepdims=True)
        weights = weights.astype(BF16)
        inverse = 1.0 / jnp.maximum(l, 1.0)
        if b == 0:
            pack_z(m * scale, l)
            leave_z(jnp.dot(weights, vt[0], preferred_element_type=F32) * inverse)
            scores = following
            continue
        pack(b, m * scale, l)
        step = RANK // 2 if b == LAST else RANK
        for c in range(0, RANK, step):
            total = jnp.dot(weights, vt[b, :, c:c + step], preferred_element_type=F32)
            d1s[b, :, c:c + step] = (total * inverse).astype(BF16)
            for d in (2, 1, 3):
                i = ys(d)
                if c == 0:
                    send(t1s.at[b, i], t1.at[b, y], sent.at[5], r_t1.at[b], at_y(i))
                cols = pl.ds(c, step)
                send(
                    d1s.at[b, yrows(i), cols], d1.at[b, y, :, cols],
                    sent.at[4], r_d1.at[b], at_y(i),
                )
        scores = following
    for b in range(1, B):
        join(b)
    join_z()
    wide[...] = jnp.zeros(wide.shape, F32)
    lat[LAST * HL:] = jnp.zeros((HL, RANK), F32)
    pieces = wo.shape[1] // LANES

    def values(part):
        latent = lat[...].astype(BF16)
        heads = jnp.zeros((ROWS, VH), F32)
        for h in range(HL):
            product = jnp.dot(latent, wuv[h], preferred_element_type=F32)
            heads = jnp.where(head == h, product, heads)
        fall[part, s] = heads.astype(BF16)
        for d in (4, 3, 5, 2, 6, 1, 7):
            send(fall.at[part, s], fall.at[part, s], sent.at[8], r_f.at[part], at_s(ss(d)))

    def project(part, some):
        arrive(fall.at[part, pl.ds(1, NS - 1)], r_f.at[part])
        ff[part] = fall[part].astype(F32).reshape(NS * ROWS, VH)
        x = [
            jnp.concatenate(
                [ff[part, pl.ds(b * HL + h, NS, stride=ROWS)] for h in range(HL)], axis=1
            )
            for b in some
        ]
        product = jnp.dot(
            jnp.concatenate(x, axis=0).astype(BF16), wo[...], preferred_element_type=F32
        )
        first, count = some[0] * NS, len(some) * NS
        for j in range(pieces):
            wide[pl.ds(first * 8 + j, count, stride=8)] = product[:, j * LANES:(j + 1) * LANES]
        rows = wide[first * 8:(first + count) * 8]
        h2s[first:first + count] = rows.reshape(count, 8, LANES).astype(BF16)

        def give(b, dz):
            i = zs(dz)
            to = {"kv": i * NY + b, "seq": s}
            send(h2s.at[b * NZ + i], h2.at[kv], sent.at[9], r_h2, to)

        for dz in FAR_FIRST:
            for b in some:
                give(b, dz)
        for b in some:
            pl.when(y != b)(functools.partial(give, b, 0))

    for b in range(1, LAST):
        finish(b)
    finish_z()
    late[0].wait()
    values(0)
    finish(LAST)
    values(1)
    late[1].wait()
    project(0, range(LAST))
    project(1, [LAST])
    h2[kv] = h2s[y * NZ + z]
    arrive(h2.at[pl.ds(1, NZ * NY - 1)], r_h2)
    total = jnp.sum(h2[...].astype(F32), axis=0)
    out[...] = jnp.concatenate([total[j:j + 1] for j in range(pieces)], axis=1).astype(
        BF16
    )
    all_sent = [
        g1r.at[pl.ds(1, NZ - 1)],
        g1.at[pl.ds(1, NZ - 1), pl.ds(0, LAST)],
        qall.at[pl.ds(0, LAST), pl.ds(0, HEADS - GROUP)],
        qrope.at[pl.ds(0, HEADS - GROUP)],
        d1s.at[pl.ds(1, LAST), pl.ds(0, HEADS - GROUP)],
        t1s.at[pl.ds(1, LAST), pl.ds(1, NY - 1)],
        d2s.at[pl.ds(1, LAST), pl.ds(1, NZ - 1)],
        t2s.at[pl.ds(1, LAST), pl.ds(1, NZ - 1)],
        fall.at[:, pl.ds(1, NS - 1)],
        h2s.at[pl.ds(1, NZ * NY - 1)],
        ya.at[pl.ds(1, NY - 1)],
        za.at[pl.ds(1, NZ - 1)],
        u1s.at[pl.ds(1, NZ - 1)],
        e1s.at[pl.ds(1, NZ - 1)],
        u2.at[pl.ds(1, NY - 1)],
        e2s.at[pl.ds(1, NY - 1)],
    ]
    for i, ref in enumerate(all_sent):
        bytes_of(ref, sent.at[i]).wait_send()


def per_device(kv_cache, lengths, q_nope, q_rope, w_uk, w_uv, w_o):
    ctx = kv_cache.shape[1]
    dmodel = w_o.shape[1]
    dma = pltpu.SemaphoreType.DMA
    anywhere = pl.BlockSpec(memory_space=pl.ANY)
    return pl.pallas_call(
        kernel,
        out_shape=jax.ShapeDtypeStruct((1, dmodel), BF16),
        in_specs=[anywhere] * 7,
        out_specs=pl.BlockSpec(memory_space=pltpu.VMEM),
        scratch_shapes=[
            pltpu.SMEM((B,), jnp.int32),
            pltpu.VMEM((B, HL, NOPE), BF16),
            pltpu.VMEM((B, HL, ROPE), BF16),
            pltpu.VMEM((B, RANK + ROPE, ctx), BF16),
            pltpu.VMEM((B, ctx, RANK), BF16),
            pltpu.VMEM((HL, NOPE, RANK), BF16),
            pltpu.VMEM((HL, RANK, VH), BF16),
            pltpu.VMEM((HL * VH, dmodel), BF16),
            pltpu.VMEM((ROWS * PARTS, LANES), F32),
            pltpu.VMEM((NZ, B, HL * PARTS, LANES), BF16),
            pltpu.VMEM((NZ, ROWS, LANES), BF16),
            pltpu.VMEM((NY, 2, ROWS, LANES), BF16),
            pltpu.VMEM((NZ, ROWS, RANK + LANES), BF16),
            pltpu.VMEM((B, GROUP * PARTS, LANES), F32),
            pltpu.VMEM((NY * ROWS, LANES), F32),
            pltpu.VMEM((B, HEADS, RANK), BF16),
            pltpu.VMEM((HEADS, B * ROPE), BF16),
            pltpu.VMEM((HEADS, LANES), BF16),
            pltpu.VMEM((NZ, ROWS, RANK), BF16),
            pltpu.VMEM((NZ, ROWS, RANK), BF16),
            pltpu.VMEM((NZ, 1, LANES), F32),
            pltpu.VMEM((NZ, 1, LANES), F32),
            pltpu.VMEM((NZ * ROWS, LANES), F32),
            pltpu.VMEM((NY * ROWS, LANES), F32),
            pltpu.VMEM((NY, ROWS, LANES), BF16),
            pltpu.VMEM((NY, ROWS, LANES), BF16),
            pltpu.VMEM((1, LANES), F32),
            pltpu.VMEM((NY, 1, LANES), F32),
            pltpu.VMEM((B, HEADS, RANK), BF16),
            pltpu.VMEM((B, NY, GROUP, RANK), BF16),
            pltpu.VMEM((B, HEADS, LANES), F32),
            pltpu.VMEM((B, NY, NZ, LANES), F32),
            pltpu.VMEM((B, NY, NZ, LANES), F32),
            pltpu.VMEM((B, NY, GROUP, LANES), F32),
            pltpu.VMEM((B, GROUP * PARTS, LANES), F32),
            pltpu.VMEM((B, NZ, ROWS, LANES), BF16),
            pltpu.VMEM((B, NZ, ROWS, LANES), BF16),
            pltpu.VMEM((B, NZ, 1, LANES), F32),
            pltpu.VMEM((B, NZ, 1, LANES), F32),
            pltpu.VMEM((B, NZ * ROWS, LANES), F32),
            pltpu.VMEM((ROWS, RANK), F32),
            pltpu.VMEM((2, NS, ROWS, VH), BF16),
            pltpu.VMEM((2, NS * ROWS, VH), F32),
            pltpu.VMEM((SEQS * 8, LANES), F32),
            pltpu.VMEM((SEQS, 8, LANES), BF16),
            pltpu.VMEM((SEQS, 8, LANES), BF16),
            dma((6,)), dma((B,)), dma((16,)),
            dma((3,)), dma((B,)), dma((2,)), dma((4,)),
            dma((B,)), dma((B,)), dma((B,)), dma((B,)),
            dma((2,)), dma,
        ],
        compiler_params=pltpu.CompilerParams(
            collective_id=0, has_side_effects=True, vmem_limit_bytes=62 * 1024 * 1024
        ),
    )(lengths, q_nope, q_rope, jnp.swapaxes(kv_cache, 1, 2), w_uk, w_uv, w_o)


def solution(mesh):
    return jax.shard_map(
        per_device,
        mesh=mesh,
        in_specs=(
            P("seq", "kv", None),
            P("seq"),
            P("seq", "kv", None),
            P("seq", "kv", None),
            P("kv", None, None),
            P("kv", None, None),
            P("kv", "seq"),
        ),
        out_specs=P("kv", "seq"),
        check_vma=False,
    )
```

```python
import functools
import math

import jax
import jax.numpy as jnp
from jax import lax
from jax.experimental import pallas as pl
from jax.experimental.pallas import tpu as pltpu
from jax.sharding import PartitionSpec as P

F32 = jnp.float32
BF16 = jnp.bfloat16
NZ, NY, NS = 8, 4, 8
B, HL = 4, 4
LAST = B - 1
SEQS = NS * B
RANK, ROPE, NOPE, VH = 512, 64, 128, 128
ROWS = B * HL
GROUP = NZ * HL
HEADS = NY * GROUP
LANES = 128
PARTS = RANK // LANES
DEAD, FLOOR = -1e30, -1e29
FAR_FIRST = sorted(range(1, NZ), key=lambda d: (-min(d, NZ - d), d))


def halves(a, c):
    first = lax.broadcasted_iota(jnp.int32, a.shape, 0) < 4
    return (
        jnp.where(first, a, pltpu.roll(c, 4, 0)),
        jnp.where(first, pltpu.roll(a, 4, 0), c),
    )


def take(block, lane):
    return jnp.broadcast_to(block[:, lane:lane + 1], block.shape)


def kernel(
    lengths_hbm, qn_hbm, qr_hbm, kv_hbm, wuk_hbm, wuv_hbm, wo_hbm, out,
    lengths, qn, qr, kvt, vt, wuk, wuv, wo,
    own, g1, g1r, ya, za, spread, around, qall, qrope, qrope3, e1s, e1, u1s, u1, fz, f2, e2s, e2, u2s, u2, d1s, d1, tall, t1s, t1, factor, flat, d2s, d2, t2s, t2, deep,
    lat, fall, ff, wide, h2s, h2,
    local, local_kv, sent, r_g1, r_g2, r_a, r_e, r_d1, r_t1, r_d2, r_t2, r_f, r_h2,
):
    kv, s = lax.axis_index("kv"), lax.axis_index("seq")
    z, y = kv // NY, kv % NY
    ctx = kvt.shape[2]
    scale = 1.0 / math.sqrt(NOPE + ROPE)

    def at_z(i):
        return {"kv": i * NY + y, "seq": s}

    def at_y(i):
        return {"kv": z * NY + i, "seq": s}

    def at_s(i):
        return {"kv": kv, "seq": i}

    def zs(d):
        return lax.rem(z + d, NZ)

    def ys(d):
        return lax.rem(y + d, NY)

    def ss(d):
        return lax.rem(s + d, NS)

    barrier = pltpu.get_barrier_semaphore()
    peers = (
        [at_z(zs(d)) for d in FAR_FIRST]
        + [at_s(ss(d)) for d in range(1, NS)]
        + [at_y(ys(d)) for d in range(1, NY)]
    )
    for peer in peers:
        pl.semaphore_signal(barrier, inc=1, device_id=peer, device_id_type=pl.DeviceIdType.MESH)

    small = [
        pltpu.make_async_copy(qn_hbm, qn, local.at[0]),
        pltpu.make_async_copy(qr_hbm, qr, local.at[1]),
        pltpu.make_async_copy(wuk_hbm, wuk, local.at[2]),
    ]
    late = [
        pltpu.make_async_copy(wuv_hbm, wuv, local.at[3]),
        pltpu.make_async_copy(wo_hbm, wo, local.at[4]),
        pltpu.make_async_copy(lengths_hbm, lengths, local.at[5]),
    ]
    caches = [
        pltpu.make_async_copy(kv_hbm.at[b], kvt.at[b], local_kv.at[b]) for b in range(B)
    ]
    for copy in small:
        copy.start()

    def send(src, dst, send_sem, recv_sem, to):
        pltpu.make_async_remote_copy(
            src_ref=src, dst_ref=dst, send_sem=send_sem, recv_sem=recv_sem,
            device_id=to, device_id_type=pl.DeviceIdType.MESH,
        ).start()

    def bytes_of(ref, sem):
        return pltpu.make_async_remote_copy(
            src_ref=ref, dst_ref=ref, send_sem=sem, recv_sem=sem,
            device_id=at_z(z), device_id_type=pl.DeviceIdType.MESH,
        )

    def arrive(ref, sem):
        bytes_of(ref, sem).wait_recv()

    def yrows(i):
        return pl.ds(pl.multiple_of(i * GROUP, GROUP), GROUP)

    for copy in small:
        copy.wait()
    for copy in caches + late:
        copy.start()
    head = lax.broadcasted_iota(jnp.int32, (ROWS, 1), 0) % HL
    q16 = qn[...].astype(F32).reshape(ROWS, NOPE).astype(BF16)
    absorbed = jnp.zeros((ROWS, RANK), F32)
    for h in range(HL):
        product = jnp.dot(q16, wuk[h], preferred_element_type=F32)
        absorbed = jnp.where(head == h, product, absorbed)
    rope = qr[...].astype(F32).reshape(ROWS, ROPE)
    for j in range(PARTS):
        own[pl.ds(j, ROWS, stride=PARTS)] = absorbed[:, j * LANES:(j + 1) * LANES]
    g1[z] = own[...].astype(BF16).reshape(B, HL * PARTS, LANES)
    ya[y, 0] = g1[z, LAST]
    g1r[z] = jnp.concatenate([rope, jnp.zeros((ROWS, LANES - ROPE), F32)], axis=1).astype(BF16)
    ya[y, 1] = g1r[z]

    pl.semaphore_wait(barrier, len(peers))

    for d in FAR_FIRST:
        send(g1.at[z, 0], g1.at[z, 0], sent.at[1], r_g1.at[1], at_z(zs(d)))
    for d in (2, 1, 3):
        send(ya.at[y], ya.at[y], sent.at[10], r_a.at[0], at_y(ys(d)))
    for d in FAR_FIRST:
        send(g1r.at[z], g1r.at[z], sent.at[0], r_g1.at[0], at_z(zs(d)))
    for d in FAR_FIRST:
        rest = g1.at[z, pl.ds(1, LAST - 1)]
        send(rest, rest, sent.at[1], r_g1.at[2], at_z(zs(d)))

    def turn_cache(b):
        caches[b].wait()
        vt[b] = kvt[b, :RANK].T

    def pass_on(b):
        spread[b] = g1[:, b].astype(F32).reshape(GROUP * PARTS, LANES)
        parts = [spread[b, pl.ds(j, GROUP, stride=PARTS)] for j in range(PARTS)]
        part = qall.at[b, yrows(y)]
        part[...] = jnp.concatenate(parts, axis=1).astype(BF16)
        for d in (2, 1, 3):
            send(part, part, sent.at[2], r_g2.at[b], at_y(ys(d)))

    turn_cache(0)
    arrive(ya.at[pl.ds(1, NY - 1)], r_a.at[0])
    around[...] = ya[:, 0].astype(F32).reshape(NY * ROWS, LANES)
    parts = [around[pl.ds(j, ROWS, stride=PARTS)] for j in range(PARTS)]
    tails = [ya[i, 1].astype(F32)[8:] for i in range(NY)]
    tail = jnp.concatenate(
        [halves(tails[0], tails[1])[1], halves(tails[2], tails[3])[1]], axis=0
    )
    za[z] = jnp.concatenate(parts + [tail], axis=1).astype(BF16)
    for d in FAR_FIRST:
        send(za.at[z], za.at[z], sent.at[11], r_a.at[1], at_z(zs(d)))
    turn_cache(1)
    arrive(g1.at[pl.ds(1, NZ - 1), 0], r_g1.at[1])
    pass_on(0)
    arrive(g1r.at[pl.ds(1, NZ - 1)], r_g1.at[0])
    for k in range(0, NZ, 4):
        blocks = [g1r[k + j].astype(F32) for j in range(4)]
        for p in range(B // 2):
            rows = slice(8 * p, 8 * p + 8)
            low = halves(blocks[0][rows], blocks[1][rows])
            high = halves(blocks[2][rows], blocks[3][rows])
            pair = [jnp.concatenate([low[i], high[i]], axis=0) for i in range(2)]
            where = pl.ds(pl.multiple_of(y * GROUP + k * HL, 16), 16)
            both = pair[0] + pltpu.roll(pair[1], ROPE, 1)
            qrope[where, p * LANES:(p + 1) * LANES] = both.astype(BF16)
    part = qrope.at[yrows(y)]
    for d in (2, 1, 3):
        send(part, part, sent.at[3], r_g2.at[LAST], at_y(ys(d)))
    arrive(g1.at[pl.ds(1, NZ - 1), pl.ds(1, LAST - 1)], r_g1.at[2])
    for b in range(1, LAST):
        pass_on(b)

    for b in range(2, B):
        turn_cache(b)

    def turn():
        arrive(za.at[pl.ds(1, NZ - 1)], r_a.at[1])
        for k in range(0, NZ, 4):
            blocks = [za[k + j].astype(F32) for j in range(4)]
            for p in range(NY // 2):
                rows = slice(8 * p, 8 * p + 8)
                low = halves(blocks[0][rows], blocks[1][rows])
                high = halves(blocks[2][rows], blocks[3][rows])
                for i in range(2):
                    both = jnp.concatenate([low[i], high[i]], axis=0).astype(BF16)
                    first = (2 * p + i) * GROUP + k * HL
                    qall[LAST, first:first + 16] = both[:, :RANK]
                    qrope3[first:first + 16] = both[:, RANK:]

    even = lax.broadcasted_iota(jnp.int32, (NZ, LANES), 1) % 2 == 0

    def pack(b, maxima, totals):
        lane = lax.broadcasted_iota(jnp.int32, (HEADS, LANES), 1)
        tall[b] = jnp.where(lane == 0, maxima, jnp.where(lane == 1, totals, 0.0))
        for i in range(NY):
            block = tall[b, pl.ds(i * GROUP, NZ, stride=HL)]
            for h in range(1, HL):
                block = block + pltpu.roll(tall[b, pl.ds(i * GROUP + h, NZ, stride=HL)], 2 * h, 1)
            t1s[b, i] = block

    def pack_z(maxima, totals):
        lane = lax.broadcasted_iota(jnp.int32, (HEADS, LANES), 1)
        tall[0] = jnp.where(lane == 0, maxima, jnp.where(lane == 1, totals, 0.0))
        block = tall[0, pl.ds(0, NZ, stride=HL)]
        for r in range(1, ROWS):
            first = (r // HL) * GROUP + r % HL
            block = block + pltpu.roll(tall[0, pl.ds(first, NZ, stride=HL)], 2 * r, 1)
        for i in range(NZ):
            u1s[i] = block[i:i + 1]

    def leave_z(outputs):
        for k in range(NZ // 2):
            blocks = [outputs[i * GROUP + 8 * k:i * GROUP + 8 * k + 8] for i in range(NY)]
            low, high = halves(blocks[0], blocks[1]), halves(blocks[2], blocks[3])
            for i in range(2):
                e1s[2 * k + i] = jnp.concatenate([low[i], high[i]], axis=0).astype(BF16)
        for d in FAR_FIRST:
            i = zs(d)
            send(u1s.at[i], u1.at[z], sent.at[12], r_e.at[0], at_z(i))
            send(e1s.at[i], e1.at[z], sent.at[13], r_e.at[1], at_z(i))

    def join_z():
        u1[z] = u1s[z]
        e1[z] = e1s[z]
        arrive(u1.at[pl.ds(1, NZ - 1)], r_e.at[0])
        stats = jnp.concatenate([u1[i] for i in range(NZ)], axis=0)
        largest = jnp.broadcast_to(jnp.max(stats, axis=0, keepdims=True), stats.shape)
        factors = jnp.exp(stats - largest) * pltpu.roll(stats, LANES - 1, 1)
        summed = jnp.broadcast_to(jnp.sum(factors, axis=0, keepdims=True), stats.shape)
        shares = factors / jnp.maximum(summed, 1.0)
        u2s[...] = jnp.where(even, largest, pltpu.roll(summed, 1, 1))[:1]
        for r in range(ROWS):
            fz[pl.ds(r, NZ, stride=ROWS)] = take(shares, 2 * r)
        arrive(e1.at[pl.ds(1, NZ - 1)], r_e.at[1])
        total = 0.0
        for i in range(NZ):
            share = jnp.concatenate([fz[i * ROWS:(i + 1) * ROWS]] * PARTS, axis=1)
            total = total + share * e1[i].astype(F32)
        for j in range(PARTS):
            f2[pl.ds(j, ROWS, stride=PARTS)] = total[:, j * LANES:(j + 1) * LANES]
        e2s[...] = f2[...].astype(BF16).reshape(NY, ROWS, LANES)
        for d in (2, 1, 3):
            i = ys(d)
            send(u2s, u2.at[y], sent.at[14], r_e.at[2], at_y(i))
            send(e2s.at[i], e2.at[y], sent.at[15], r_e.at[3], at_y(i))

    def finish_z():
        u2[y] = u2s[...]
        e2[y] = e2s[y]
        arrive(u2.at[pl.ds(1, NY - 1)], r_e.at[2])
        rows = [u2[i] for i in range(NY)] + [jnp.full((NZ - NY, LANES), DEAD, F32)]
        stats = jnp.concatenate(rows, axis=0)
        stats = pltpu.roll(stats, lax.rem(LANES - 2 * HL * y, LANES), 1)
        largest = jnp.max(stats, axis=0, keepdims=True)
        factors = jnp.exp(stats - largest) * pltpu.roll(stats, LANES - 1, 1)
        summed = jnp.sum(factors, axis=0, keepdims=True)
        shares = factors / jnp.maximum(summed, 1.0)
        arrive(e2.at[pl.ds(1, NY - 1)], r_e.at[3])
        f2[...] = e2[...].astype(F32).reshape(NY * ROWS, LANES)
        for h in range(HL):
            share = take(shares, 2 * h)[:NY]
            for j in range(PARTS):
                rows = f2[pl.ds(h * PARTS + j, NY, stride=ROWS)]
                row = jnp.sum(share * rows, axis=0, keepdims=True)
                lat[h:h + 1, j * LANES:(j + 1) * LANES] = row

    def join(b):
        t1[b, y] = t1s[b, y]
        d1[b, y] = d1s[b, yrows(y)]
        arrive(t1.at[b, pl.ds(1, NY - 1)], r_t1.at[b])
        stats = [t1[b, i] for i in range(NY)]
        largest = functools.reduce(jnp.maximum, stats)
        factors = [jnp.exp(t - largest) * pltpu.roll(t, LANES - 1, 1) for t in stats]
        summed = sum(factors)
        inverse = 1.0 / jnp.maximum(summed, 1.0)
        joined = jnp.where(even, largest, pltpu.roll(summed, 1, 1))
        for i in range(NZ):
            t2s[b, i] = joined[i:i + 1]
        for d in FAR_FIRST:
            i = zs(d)
            send(t2s.at[b, i], t2.at[b, z], sent.at[7], r_t2.at[b], at_z(i))
        for i in range(NY):
            share = factors[i] * inverse
            for h in range(HL):
                factor[b, i, pl.ds(h, NZ, stride=HL)] = take(share, 2 * h)
        arrive(d1.at[b, pl.ds(1, NY - 1)], r_d1.at[b])
        total = 0.0
        for i in range(NY):
            share = jnp.concatenate([factor[b, i]] * PARTS, axis=1)
            total = total + share * d1[b, i].astype(F32)
        for j in range(PARTS):
            flat[b, pl.ds(j, GROUP, stride=PARTS)] = total[:, j * LANES:(j + 1) * LANES]
        d2s[b] = flat[b].astype(BF16).reshape(NZ, ROWS, LANES)
        for d in FAR_FIRST:
            i = zs(d)
            send(d2s.at[b, i], d2.at[b, z], sent.at[6], r_d2.at[b], at_z(i))

    def finish(b):
        t2[b, z] = t2s[b, z]
        d2[b, z] = d2s[b, z]
        arrive(t2.at[b, pl.ds(1, NZ - 1)], r_t2.at[b])
        stats = jnp.concatenate([t2[b, i] for i in range(NZ)], axis=0)
        largest = jnp.max(stats, axis=0, keepdims=True)
        factors = jnp.exp(stats - largest) * pltpu.roll(stats, LANES - 1, 1)
        summed = jnp.sum(factors, axis=0, keepdims=True)
        shares = factors / jnp.maximum(summed, 1.0)
        arrive(d2.at[b, pl.ds(1, NZ - 1)], r_d2.at[b])
        deep[b] = d2[b].astype(F32).reshape(NZ * ROWS, LANES)
        for h in range(HL):
            share = take(shares, 2 * h)
            for j in range(PARTS):
                rows = deep[b, pl.ds(h * PARTS + j, NZ, stride=ROWS)]
                row = jnp.sum(share * rows, axis=0, keepdims=True)
                lat[b * HL + h:b * HL + h + 1, j * LANES:(j + 1) * LANES] = row

    first_slot = kv * ctx
    late[2].wait()

    def scores_of(b):
        if b == LAST:
            turn()
            tail = qrope3[:, :ROPE]
        else:
            arrive(qall.at[b, pl.ds(0, HEADS - GROUP)], r_g2.at[b])
            if b == 0:
                arrive(qrope.at[pl.ds(0, HEADS - GROUP)], r_g2.at[LAST])
            tail = qrope[:, b * ROPE:(b + 1) * ROPE]
        scores = jnp.dot(
            qall[b], kvt[b, :RANK], preferred_element_type=F32
        ) + jnp.dot(tail, kvt[b, RANK:], preferred_element_type=F32)
        slot = lax.broadcasted_iota(jnp.int32, (1, ctx), 1)
        return jnp.where(slot < lengths[b] - first_slot, scores, DEAD)

    scores = scores_of(0)
    for b in range(B):
        following = scores_of(b + 1) if b + 1 < B else None
        m = jnp.max(scores, axis=1, keepdims=True)
        weights = jnp.exp2((scores - jnp.maximum(m, FLOOR)) * (scale * math.log2(math.e)))
        l = jnp.sum(weights, axis=1, keepdims=True)
        weights = weights.astype(BF16)
        inverse = 1.0 / jnp.maximum(l, 1.0)
        if b == 0:
            pack_z(m * scale, l)
            leave_z(jnp.dot(weights, vt[0], preferred_element_type=F32) * inverse)
            scores = following
            continue
        pack(b, m * scale, l)
        step = RANK // 2 if b == LAST else RANK
        for c in range(0, RANK, step):
            total = jnp.dot(weights, vt[b, :, c:c + step], preferred_element_type=F32)
            d1s[b, :, c:c + step] = (total * inverse).astype(BF16)
            for d in (2, 1, 3):
                i = ys(d)
                if c == 0:
                    send(t1s.at[b, i], t1.at[b, y], sent.at[5], r_t1.at[b], at_y(i))
                cols = pl.ds(c, step)
                send(
                    d1s.at[b, yrows(i), cols], d1.at[b, y, :, cols],
                    sent.at[4], r_d1.at[b], at_y(i),
                )
        scores = following
    for b in range(1, B):
        join(b)
    join_z()
    wide[...] = jnp.zeros(wide.shape, F32)
    lat[LAST * HL:] = jnp.zeros((HL, RANK), F32)
    pieces = wo.shape[1] // LANES

    def values(part):
        latent = lat[...].astype(BF16)
        heads = jnp.zeros((ROWS, VH), F32)
        for h in range(HL):
            product = jnp.dot(latent, wuv[h], preferred_element_type=F32)
            heads = jnp.where(head == h, product, heads)
        fall[part, s] = heads.astype(BF16)
        for d in (4, 3, 5, 2, 6, 1, 7):
            send(fall.at[part, s], fall.at[part, s], sent.at[8], r_f.at[part], at_s(ss(d)))

    def project(part, some):
        arrive(fall.at[part, pl.ds(1, NS - 1)], r_f.at[part])
        ff[part] = fall[part].astype(F32).reshape(NS * ROWS, VH)
        x = [
            jnp.concatenate(
                [ff[part, pl.ds(b * HL + h, NS, stride=ROWS)] for h in range(HL)], axis=1
            )
            for b in some
        ]
        product = jnp.dot(
            jnp.concatenate(x, axis=0).astype(BF16), wo[...], preferred_element_type=F32
        )
        first, count = some[0] * NS, len(some) * NS
        for j in range(pieces):
            wide[pl.ds(first * 8 + j, count, stride=8)] = product[:, j * LANES:(j + 1) * LANES]
        rows = wide[first * 8:(first + count) * 8]
        h2s[first:first + count] = rows.reshape(count, 8, LANES).astype(BF16)

        def give(b, dz):
            i = zs(dz)
            to = {"kv": i * NY + b, "seq": s}
            send(h2s.at[b * NZ + i], h2.at[kv], sent.at[9], r_h2, to)

        for dz in FAR_FIRST:
            for b in some:
                give(b, dz)
        for b in some:
            pl.when(y != b)(functools.partial(give, b, 0))

    for b in range(1, LAST):
        finish(b)
    finish_z()
    late[0].wait()
    values(0)
    finish(LAST)
    values(1)
    late[1].wait()
    project(0, range(LAST))
    project(1, [LAST])
    h2[kv] = h2s[y * NZ + z]
    all_sent = [
        g1r.at[pl.ds(1, NZ - 1)],
        g1.at[pl.ds(1, NZ - 1), pl.ds(0, LAST)],
        qall.at[pl.ds(0, LAST), pl.ds(0, HEADS - GROUP)],
        qrope.at[pl.ds(0, HEADS - GROUP)],
        d1s.at[pl.ds(1, LAST), pl.ds(0, HEADS - GROUP)],
        t1s.at[pl.ds(1, LAST), pl.ds(1, NY - 1)],
        d2s.at[pl.ds(1, LAST), pl.ds(1, NZ - 1)],
        t2s.at[pl.ds(1, LAST), pl.ds(1, NZ - 1)],
        fall.at[:, pl.ds(1, NS - 1)],
        h2s.at[pl.ds(1, NZ * NY - 1)],
        ya.at[pl.ds(1, NY - 1)],
        za.at[pl.ds(1, NZ - 1)],
        u1s.at[pl.ds(1, NZ - 1)],
        e1s.at[pl.ds(1, NZ - 1)],
        u2.at[pl.ds(1, NY - 1)],
        e2s.at[pl.ds(1, NY - 1)],
    ]
    for i, ref in enumerate(all_sent):
        bytes_of(ref, sent.at[i]).wait_send()
    arrive(h2.at[pl.ds(1, NZ * NY - 1)], r_h2)
    total = jnp.sum(h2[...].astype(F32), axis=0)
    out[...] = jnp.concatenate([total[j:j + 1] for j in range(pieces)], axis=1).astype(
        BF16
    )


def per_device(kv_cache, lengths, q_nope, q_rope, w_uk, w_uv, w_o):
    ctx = kv_cache.shape[1]
    dmodel = w_o.shape[1]
    dma = pltpu.SemaphoreType.DMA
    anywhere = pl.BlockSpec(memory_space=pl.ANY)
    return pl.pallas_call(
        kernel,
        out_shape=jax.ShapeDtypeStruct((1, dmodel), BF16),
        in_specs=[anywhere] * 7,
        out_specs=pl.BlockSpec(memory_space=pltpu.VMEM),
        scratch_shapes=[
            pltpu.SMEM((B,), jnp.int32),
            pltpu.VMEM((B, HL, NOPE), BF16),
            pltpu.VMEM((B, HL, ROPE), BF16),
            pltpu.VMEM((B, RANK + ROPE, ctx), BF16),
            pltpu.VMEM((B, ctx, RANK), BF16),
            pltpu.VMEM((HL, NOPE, RANK), BF16),
            pltpu.VMEM((HL, RANK, VH), BF16),
            pltpu.VMEM((HL * VH, dmodel), BF16),
            pltpu.VMEM((ROWS * PARTS, LANES), F32),
            pltpu.VMEM((NZ, B, HL * PARTS, LANES), BF16),
            pltpu.VMEM((NZ, ROWS, LANES), BF16),
            pltpu.VMEM((NY, 2, ROWS, LANES), BF16),
            pltpu.VMEM((NZ, ROWS, RANK + LANES), BF16),
            pltpu.VMEM((B, GROUP * PARTS, LANES), F32),
            pltpu.VMEM((NY * ROWS, LANES), F32),
            pltpu.VMEM((B, HEADS, RANK), BF16),
            pltpu.VMEM((HEADS, B * ROPE), BF16),
            pltpu.VMEM((HEADS, LANES), BF16),
            pltpu.VMEM((NZ, ROWS, RANK), BF16),
            pltpu.VMEM((NZ, ROWS, RANK), BF16),
            pltpu.VMEM((NZ, 1, LANES), F32),
            pltpu.VMEM((NZ, 1, LANES), F32),
            pltpu.VMEM((NZ * ROWS, LANES), F32),
            pltpu.VMEM((NY * ROWS, LANES), F32),
            pltpu.VMEM((NY, ROWS, LANES), BF16),
            pltpu.VMEM((NY, ROWS, LANES), BF16),
            pltpu.VMEM((1, LANES), F32),
            pltpu.VMEM((NY, 1, LANES), F32),
            pltpu.VMEM((B, HEADS, RANK), BF16),
            pltpu.VMEM((B, NY, GROUP, RANK), BF16),
            pltpu.VMEM((B, HEADS, LANES), F32),
            pltpu.VMEM((B, NY, NZ, LANES), F32),
            pltpu.VMEM((B, NY, NZ, LANES), F32),
            pltpu.VMEM((B, NY, GROUP, LANES), F32),
            pltpu.VMEM((B, GROUP * PARTS, LANES), F32),
            pltpu.VMEM((B, NZ, ROWS, LANES), BF16),
            pltpu.VMEM((B, NZ, ROWS, LANES), BF16),
            pltpu.VMEM((B, NZ, 1, LANES), F32),
            pltpu.VMEM((B, NZ, 1, LANES), F32),
            pltpu.VMEM((B, NZ * ROWS, LANES), F32),
            pltpu.VMEM((ROWS, RANK), F32),
            pltpu.VMEM((2, NS, ROWS, VH), BF16),
            pltpu.VMEM((2, NS * ROWS, VH), F32),
            pltpu.VMEM((SEQS * 8, LANES), F32),
            pltpu.VMEM((SEQS, 8, LANES), BF16),
            pltpu.VMEM((SEQS, 8, LANES), BF16),
            dma((6,)), dma((B,)), dma((16,)),
            dma((3,)), dma((B,)), dma((2,)), dma((4,)),
            dma((B,)), dma((B,)), dma((B,)), dma((B,)),
            dma((2,)), dma,
        ],
        compiler_params=pltpu.CompilerParams(
            collective_id=0, has_side_effects=True, vmem_limit_bytes=62 * 1024 * 1024
        ),
    )(lengths, q_nope, q_rope, jnp.swapaxes(kv_cache, 1, 2), w_uk, w_uv, w_o)


def solution(mesh):
    return jax.shard_map(
        per_device,
        mesh=mesh,
        in_specs=(
            P("seq", "kv", None),
            P("seq"),
            P("seq", "kv", None),
            P("seq", "kv", None),
            P("kv", None, None),
            P("kv", None, None),
            P("kv", "seq"),
        ),
        out_specs=P("kv", "seq"),
        check_vma=False,
    )
```
